256 devices in a mesh: seq: 16 (over x, z_hi), res: 16 (over y, z_lo, core).
Axes of the slice: x: 4, y: 4, z: 8 (z_hi: 4, z_lo: 2; z = z_hi * 2 + z_lo), core: 2. Of those that a mesh axis runs over, the one named last changes fastest.
Arguments:
- aligned_stack: bfloat16 [256, 512, 768], P('seq', 'res'), may hold values from -8 to 8
- asking_projector: bfloat16 [768, 768], replicated, may hold values from -0.25 to 0.25
- lookup_projector: bfloat16 [768, 768], replicated, may hold values from -0.25 to 0.25
- content_projector: bfloat16 [768, 768], replicated, may hold values from -0.21875 to 0.21875
- final_projector: bfloat16 [768, 768], replicated, may hold values from -0.21875 to 0.21875
Outputs:
- mixed: bfloat16 [256, 512, 768], P('seq', 'res')
The draws below stay inside these ranges and needn't reach their ends.
All inputs are finite; a program needn't handle non-finite values.
Results may differ from the reference program's by a relative error of at most 0.0075.
Values may be sent and summed in bfloat16 or wider, within the bound.
No kernel may reach another device: no remote copies, remote signals or barrier semaphores. Data moves between devices by JAX's collectives and lax.ppermute only.
A program may use at most 128 MiB of HBM per device.

```python
import math
import jax
import jax.numpy as jnp

D = 768
HEADS = 12
HEAD = 64
ROWS = 256
RES = 512


def draw_asking_projector(key, part):
    key = jax.random.fold_in(key, 21)
    matrix = jax.random.normal(key, (D, D), jnp.float32)
    return jnp.clip(matrix * D ** (-0.5), -0.25, 0.25).astype(jnp.bfloat16)


def draw_lookup_projector(key, part):
    key = jax.random.fold_in(key, 22)
    matrix = jax.random.normal(key, (D, D), jnp.float32)
    return jnp.clip(matrix * D ** (-0.5), -0.25, 0.25).astype(jnp.bfloat16)


def draw_aligned_stack(key, part):
    key = jax.random.fold_in(key, 7)
    first_key = jax.random.fold_in(key, 0)
    noise = jnp.clip(jax.random.normal(first_key, (ROWS, RES, D), jnp.float32), -6.0, 6.0)
    return noise.astype(jnp.bfloat16)


def centred(key, extent, width, reach, kind=jnp.bfloat16):
    entries = jax.random.normal(key, extent, jnp.float32) * width
    return jnp.minimum(jnp.maximum(entries, -reach), reach).astype(kind)


def setup_inputs(seed: int = 0) -> dict:
    splits = jax.random.split(jax.random.key(seed), 6)
    return {
        "aligned_stack": draw_aligned_stack(jax.random.fold_in(splits[5], 71), 0),
        "asking_projector": draw_asking_projector(jax.random.fold_in(splits[5], 71), 0),
        "lookup_projector": draw_lookup_projector(jax.random.fold_in(splits[5], 71), 0),
        "content_projector": centred(splits[3], (D, D), D ** -0.5, 0.21875),
        "final_projector": centred(splits[4], (D, D), D ** -0.5, 0.21875),
    }


def project(merged_lines, weight, chain_total, column_total, factor):
    product = jnp.dot(merged_lines, weight, preferred_element_type=jnp.float32) * factor
    return product.astype(jnp.bfloat16).reshape(chain_total, column_total, HEADS, HEAD)

def reference(aligned_stack, asking_projector, lookup_projector, content_projector, final_projector):
    chain_total, column_total, channel_depth = aligned_stack.shape
    merged_lines = aligned_stack.reshape(chain_total * column_total, channel_depth)
    factor = 1.0 / (math.sqrt(HEAD) * math.sqrt(chain_total))
    queries = project(merged_lines, asking_projector, chain_total, column_total, factor)
    keys = project(merged_lines, lookup_projector, chain_total, column_total, 1.0)
    values = project(merged_lines, content_projector, chain_total, column_total, 1.0)
    logits = jnp.einsum('rihd,rjhd->hij', queries.astype(jnp.float32), keys.astype(jnp.float32))
    weights = jax.nn.softmax(logits, axis=-1).astype(jnp.bfloat16)
    attended = jnp.einsum('hij,rjhd->rihd', weights.astype(jnp.float32), values.astype(jnp.float32))
    attended = attended.astype(jnp.bfloat16).reshape(chain_total * column_total, channel_depth)
    mixed = merged_lines.astype(jnp.float32) + jnp.dot(attended, final_projector, preferred_element_type=jnp.float32)
    return mixed.astype(jnp.bfloat16).reshape(chain_total, column_total, channel_depth)
```

```python
import functools
import math

import jax
import jax.numpy as jnp
from jax import lax
from jax.experimental import pallas as pl
from jax.experimental.pallas import tpu as pltpu
from jax.sharding import Mesh, PartitionSpec as P

HEADS = 12
HEAD = 64
GROUPS = 4
SLOTS = 3
F32 = jnp.float32
BF16 = jnp.bfloat16
PARAMS = pltpu.CompilerParams(vmem_limit_bytes=48 * 1024 * 1024)


def place(head):
    return (head // 2, head % 2) if head < 8 else (head - 8, 2)


def low_lanes(shape):
    return lax.broadcasted_iota(jnp.int32, shape, len(shape) - 1) < HEAD


def project_kernel(factors, lines_ref, *refs):
    count = len(factors)
    weights, outs = refs[:count], refs[count:]
    rows, cols = 16, 32
    for weight_ref, out_ref, factor in zip(weights, outs, factors):
        for half in range(3):
            product = jnp.dot(
                lines_ref[...],
                weight_ref[:, 256 * half : 256 * half + 256],
                preferred_element_type=F32,
            )
            if factor != 1.0:
                product = product * factor
            product = product.reshape(rows, cols, 256)
            for part in range(2):
                pair = 2 * half + part
                tile = product[:, :, 128 * part : 128 * part + 128].reshape(rows // 2, 2, cols, 128)
                first, second = tile[:, 0], tile[:, 1]
                low = low_lanes(first.shape)
                ends = (
                    jnp.where(low, first, pltpu.roll(second, HEAD, 2)),
                    jnp.where(low, pltpu.roll(first, HEAD, 2), second),
                )
                for side in range(2):
                    group, slot = place(2 * pair + side)
                    for step in range(rows // 2):
                        out_ref[group, slot, :, 128 * step : 128 * step + 128] = ends[side][
                            step
                        ].astype(BF16)


def project(lines, weights, factors):
    shape = jax.ShapeDtypeStruct((GROUPS, SLOTS, 32, 1024), BF16)
    return pl.pallas_call(
        functools.partial(project_kernel, factors),
        out_shape=[shape] * len(weights),
        compiler_params=PARAMS,
        cost_estimate=pl.CostEstimate(
            flops=2 * 512 * 768 * 768 * len(weights),
            bytes_accessed=4 * 786432 * len(weights),
            transcendentals=0,
        ),
    )(lines, *weights)


def logits_kernel(queries_ref, *refs):
    keys, out_ref = refs[:4], refs[4]
    for slot in range(SLOTS):
        query = queries_ref[:, slot].reshape(128, 1024)
        key = jnp.concatenate([k[:, slot].reshape(128, 1024) for k in keys], axis=0)
        scores = lax.dot_general(
            query, key, (((1,), (1,)), ((), ())), preferred_element_type=F32
        )
        out_ref[:, slot] = scores.reshape(16, 8, 512)


def logits(queries, keys):
    return pl.pallas_call(
        logits_kernel,
        out_shape=jax.ShapeDtypeStruct((16, SLOTS, 8, 512), F32),
        compiler_params=PARAMS,
        cost_estimate=pl.CostEstimate(
            flops=2 * 3 * 128 * 512 * 1024, bytes_accessed=5 * 786432, transcendentals=0
        ),
    )(queries, *keys)


def softmax_kernel(terms_ref, out_ref):
    total = jnp.sum(terms_ref[...], axis=0)
    top = jnp.max(total, axis=-1, keepdims=True)
    grown = jnp.exp(total - top)
    share = grown / jnp.sum(grown, axis=-1, keepdims=True)
    share = jnp.concatenate([share[:, :, :256], share[:, :, 256:]], axis=1).astype(BF16)
    out_ref[...] = jnp.broadcast_to(share[None], out_ref.shape)


def softmax(terms):
    return pl.pallas_call(
        softmax_kernel,
        out_shape=jax.ShapeDtypeStruct((16, SLOTS, 16, 256), BF16),
        compiler_params=PARAMS,
    )(terms)


def attend_kernel(shares_ref, *refs):
    values, out_ref = refs[:4], refs[4]
    for slot in range(SLOTS):
        share = shares_ref[:, slot].astype(F32).reshape(16, 2, 8, 256)
        share = jnp.concatenate([share[:, 0], share[:, 1]], axis=-1).reshape(128, 512).astype(BF16)
        value = jnp.concatenate([v[:, slot].reshape(128, 1024) for v in values], axis=0)
        mixed = jnp.dot(share, value, preferred_element_type=F32)
        out_ref[:, slot] = mixed.astype(BF16).reshape(4, 32, 1024)


def attend(shares, values):
    return pl.pallas_call(
        attend_kernel,
        out_shape=jax.ShapeDtypeStruct((GROUPS, SLOTS, 32, 1024), BF16),
        compiler_params=PARAMS,
        cost_estimate=pl.CostEstimate(
            flops=2 * 3 * 128 * 512 * 1024, bytes_accessed=5 * 786432, transcendentals=0
        ),
    )(shares, *values)


def finish_kernel(attended_ref, lines_ref, weight_ref, out_ref, joined_ref):
    rows, cols = 16, 32
    for pair in range(HEADS // 2):
        ends = []
        for side in range(2):
            group, slot = place(2 * pair + side)
            ends.append(attended_ref[group, slot].astype(F32))
        for step in range(rows // 2):
            left, right = (end[:, 128 * step : 128 * step + 128] for end in ends)
            low = low_lanes(left.shape)
            first = jnp.where(low, left, pltpu.roll(right, HEAD, 1))
            second = jnp.where(low, pltpu.roll(left, HEAD, 1), right)
            at = 2 * step * cols
            lanes = slice(128 * pair, 128 * pair + 128)
            joined_ref[at : at + cols, lanes] = first.astype(BF16)
            joined_ref[at + cols : at + 2 * cols, lanes] = second.astype(BF16)
    for part in range(3):
        lanes = slice(256 * part, 256 * part + 256)
        product = jnp.dot(joined_ref[...], weight_ref[:, lanes], preferred_element_type=F32)
        out_ref[:, lanes] = (lines_ref[:, lanes].astype(F32) + product).astype(BF16)


def finish(attended, lines, weight):
    return pl.pallas_call(
        finish_kernel,
        out_shape=jax.ShapeDtypeStruct((512, 768), BF16),
        scratch_shapes=[pltpu.VMEM((512, 768), BF16)],
        compiler_params=PARAMS,
    )(attended, lines, weight)


def swap(array, axis):
    return lax.ppermute(array, axis, [(0, 1), (1, 0)])


def exchange(array, axes):
    return lax.all_to_all(array, axes, 0, 0, tiled=True)


def spread(array):
    far = swap(array, "zl")
    return array, swap(array, "c"), far, swap(far, "c")


def on_device(stack, asking, lookup, content, final):
    chains, columns, depth = stack.shape
    lines = stack.reshape(chains * columns, depth)
    factor = 1.0 / (math.sqrt(HEAD) * math.sqrt(256))
    (keys,) = project(lines, [lookup], (1.0,))
    keys = spread(exchange(keys, "y"))
    queries, values = project(lines, [asking, content], (factor, 1.0))
    queries = exchange(queries, "y")
    values = spread(exchange(values, "y"))
    terms = exchange(logits(queries, keys), ("x", "zh"))
    shares = exchange(softmax(terms), ("x", "zh"))
    attended = exchange(attend(shares, values), "y")
    return finish(attended, lines, final).reshape(chains, columns, depth)


def solution(mesh):
    fine = Mesh(mesh.devices.reshape(4, 4, 4, 2, 2), ("x", "zh", "y", "zl", "c"))
    spec = P(("x", "zh"), ("y", "zl", "c"), None)
    return jax.shard_map(
        on_device,
        mesh=fine,
        in_specs=(spec, P(), P(), P(), P()),
        out_specs=spec,
        check_vma=False,
    )
```

```python
import functools
import math

import jax
import jax.numpy as jnp
from jax import lax
from jax.experimental import pallas as pl
from jax.experimental.pallas import tpu as pltpu
from jax.sharding import Mesh, PartitionSpec as P

HEADS = 12
HEAD = 64
GROUPS = 4
SLOTS = 3
F32 = jnp.float32
BF16 = jnp.bfloat16
PARAMS = pltpu.CompilerParams(vmem_limit_bytes=48 * 1024 * 1024)


def place(head):
    return (head // 2, head % 2) if head < 8 else (head - 8, 2)


def low_lanes(shape):
    return lax.broadcasted_iota(jnp.int32, shape, len(shape) - 1) < HEAD


def project_kernel(factors, lines_ref, *refs):
    out_ref = refs[-1]
    rows, cols = 16, 32
    for item, (weight_ref, factor) in enumerate(zip(refs, factors)):
        for half in range(3):
            product = jnp.dot(
                lines_ref[...],
                weight_ref[:, 256 * half : 256 * half + 256],
                preferred_element_type=F32,
            )
            if factor != 1.0:
                product = product * factor
            product = product.reshape(rows, cols, 256)
            for part in range(2):
                pair = 2 * half + part
                tile = product[:, :, 128 * part : 128 * part + 128].reshape(rows // 2, 2, cols, 128)
                first, second = tile[:, 0], tile[:, 1]
                low = low_lanes(first.shape)
                ends = (
                    jnp.where(low, first, pltpu.roll(second, HEAD, 2)),
                    jnp.where(low, pltpu.roll(first, HEAD, 2), second),
                )
                for side in range(2):
                    group, slot = place(2 * pair + side)
                    for step in range(rows // 2):
                        lanes = slice(128 * step, 128 * step + 128)
                        out_ref[group, item, slot, :, lanes] = ends[side][step].astype(BF16)


def project(lines, weights, factors):
    return pl.pallas_call(
        functools.partial(project_kernel, factors),
        out_shape=jax.ShapeDtypeStruct((GROUPS, len(weights), SLOTS, 32, 1024), BF16),
        compiler_params=PARAMS,
        cost_estimate=pl.CostEstimate(
            flops=2 * 512 * 768 * 768 * len(weights),
            bytes_accessed=4 * 786432 * len(weights),
            transcendentals=0,
        ),
    )(lines, *weights)


def block(ref, item, slot):
    return ref[:, item, slot].reshape(128, 1024)


def logits_kernel(queries_ref, *refs):
    keys, out_ref = refs[:4], refs[4]
    for slot in range(SLOTS):
        key = jnp.concatenate([block(k, 0, slot) for k in keys], axis=0)
        scores = lax.dot_general(
            block(queries_ref, 0, slot),
            key,
            (((1,), (1,)), ((), ())),
            preferred_element_type=F32,
        )
        out_ref[:, slot] = scores.reshape(4, 32, 512)


def logits(queries, keys):
    return pl.pallas_call(
        logits_kernel,
        out_shape=jax.ShapeDtypeStruct((4, SLOTS, 32, 512), F32),
        compiler_params=PARAMS,
        cost_estimate=pl.CostEstimate(
            flops=2 * 3 * 128 * 512 * 1024, bytes_accessed=5 * 786432, transcendentals=0
        ),
    )(queries, *keys)


def reduce_kernel(terms_ref, out_ref):
    total = jnp.sum(terms_ref[...], axis=0).astype(BF16)
    out_ref[...] = jnp.broadcast_to(total[None], out_ref.shape)


def softmax_kernel(terms_ref, out_ref):
    total = jnp.sum(terms_ref[...].astype(F32), axis=0)
    top = jnp.max(total, axis=-1, keepdims=True)
    grown = jnp.exp(total - top)
    share = (grown / jnp.sum(grown, axis=-1, keepdims=True)).astype(BF16)
    out_ref[...] = jnp.broadcast_to(share[None], out_ref.shape)


def copies(kernel, terms):
    return pl.pallas_call(
        kernel,
        out_shape=jax.ShapeDtypeStruct((4, SLOTS, 32, 512), BF16),
        compiler_params=PARAMS,
    )(terms)


def attend_kernel(shares_ref, values_ref, *refs):
    values, out_ref = refs[:3], refs[3]
    for slot in range(SLOTS):
        share = shares_ref[:, slot].reshape(128, 512)
        value = [block(values_ref, 1, slot)] + [block(v, 0, slot) for v in values]
        mixed = jnp.dot(share, jnp.concatenate(value, axis=0), preferred_element_type=F32)
        out_ref[:, slot] = mixed.astype(BF16).reshape(4, 32, 1024)


def attend(shares, values):
    return pl.pallas_call(
        attend_kernel,
        out_shape=jax.ShapeDtypeStruct((GROUPS, SLOTS, 32, 1024), BF16),
        compiler_params=PARAMS,
        cost_estimate=pl.CostEstimate(
            flops=2 * 3 * 128 * 512 * 1024, bytes_accessed=5 * 786432, transcendentals=0
        ),
    )(shares, *values)


def finish_kernel(attended_ref, lines_ref, weight_ref, out_ref, joined_ref):
    rows, cols = 16, 32
    for pair in range(HEADS // 2):
        ends = []
        for side in range(2):
            group, slot = place(2 * pair + side)
            ends.append(attended_ref[group, slot].astype(F32))
        for step in range(rows // 2):
            left, right = (end[:, 128 * step : 128 * step + 128] for end in ends)
            low = low_lanes(left.shape)
            first = jnp.where(low, left, pltpu.roll(right, HEAD, 1))
            second = jnp.where(low, pltpu.roll(left, HEAD, 1), right)
            at = 2 * step * cols
            lanes = slice(128 * pair, 128 * pair + 128)
            joined_ref[at : at + cols, lanes] = first.astype(BF16)
            joined_ref[at + cols : at + 2 * cols, lanes] = second.astype(BF16)
    for part in range(3):
        lanes = slice(256 * part, 256 * part + 256)
        product = jnp.dot(joined_ref[...], weight_ref[:, lanes], preferred_element_type=F32)
        out_ref[:, lanes] = (lines_ref[:, lanes].astype(F32) + product).astype(BF16)


def finish(attended, lines, weight):
    return pl.pallas_call(
        finish_kernel,
        out_shape=jax.ShapeDtypeStruct((512, 768), BF16),
        scratch_shapes=[pltpu.VMEM((512, 768), BF16)],
        compiler_params=PARAMS,
    )(attended, lines, weight)


def swap(array, axis):
    return lax.ppermute(array, axis, [(0, 1), (1, 0)])


def exchange(array, axes):
    return lax.all_to_all(array, axes, 0, 0, tiled=True)


def spread(array):
    far = swap(array, "zl")
    return swap(array, "c"), far, swap(far, "c")


def on_device(stack, asking, lookup, content, final):
    chains, columns, depth = stack.shape
    lines = stack.reshape(chains * columns, depth)
    factor = 1.0 / (math.sqrt(HEAD) * math.sqrt(256))
    keys = exchange(project(lines, [lookup], (1.0,)), "y")
    both = exchange(project(lines, [asking, content], (factor, 1.0)), "y")
    terms = exchange(logits(both, (keys, *spread(keys))), "x")
    values = (both, *spread(both[:, 1:]))
    terms = exchange(copies(reduce_kernel, terms), "zh")
    shares = exchange(copies(softmax_kernel, terms), "x")
    attended = exchange(attend(shares, values), "y")
    return finish(attended, lines, final).reshape(chains, columns, depth)


def solution(mesh):
    fine = Mesh(mesh.devices.reshape(4, 4, 4, 2, 2), ("x", "zh", "y", "zl", "c"))
    spec = P(("x", "zh"), ("y", "zl", "c"), None)
    return jax.shard_map(
        on_device,
        mesh=fine,
        in_specs=(spec, P(), P(), P(), P()),
        out_specs=spec,
        check_vma=False,
    )
```

```python
import functools
import math

import jax
import jax.numpy as jnp
from jax import lax
from jax.experimental import pallas as pl
from jax.experimental.pallas import tpu as pltpu
from jax.sharding import Mesh, PartitionSpec as P

HEADS = 12
HEAD = 64
GROUPS = 4
SLOTS = 3
F32 = jnp.float32
BF16 = jnp.bfloat16
PARAMS = pltpu.CompilerParams(vmem_limit_bytes=20 * 1024 * 1024)
ALL_VMEM = pltpu.CompilerParams(vmem_limit_bytes=62 * 1024 * 1024)


def place(head):
    return (head // 2, head % 2) if head < 8 else (head - 8, 2)


def low_lanes(shape):
    return lax.broadcasted_iota(jnp.int32, shape, len(shape) - 1) < HEAD


def lay_out(lines, weight, factor, half, store):
    rows, cols = 16, 32
    product = jnp.dot(lines, weight, preferred_element_type=F32)
    if factor != 1.0:
        product = product * factor
    product = product.reshape(rows, cols, 256)
    for part in range(2):
        pair = 2 * half + part
        tile = product[:, :, 128 * part : 128 * part + 128].reshape(rows // 2, 2, cols, 128)
        first, second = tile[:, 0], tile[:, 1]
        low = low_lanes(first.shape)
        ends = (
            jnp.where(low, first, pltpu.roll(second, HEAD, 2)),
            jnp.where(low, pltpu.roll(first, HEAD, 2), second),
        )
        for side in range(2):
            group, slot = place(2 * pair + side)
            for step in range(rows // 2):
                lanes = slice(128 * step, 128 * step + 128)
                store(group, slot, lanes, ends[side][step].astype(BF16))


def project_kernel(factors, lines_ref, *refs):
    out_ref, mark_ref = refs[-2:]
    mark_ref[...] = jnp.zeros_like(mark_ref)
    for half in range(3):

        @pl.when(pl.program_id(0) == half)
        def _(half=half):
            for item, (weight_ref, factor) in enumerate(zip(refs, factors)):

                def store(group, slot, lanes, part, item=item):
                    out_ref[group, item * SLOTS + slot, :, lanes] = part

                lay_out(lines_ref[...], weight_ref[...], factor, half, store)


def project(lines, weights, factors, *marks):
    count = len(weights)
    shape = (GROUPS, count * SLOTS, 32, 1024)
    whole = pl.BlockSpec(lines.shape, lambda i: (0, 0))
    small = pl.BlockSpec((8, 128), lambda i: (0, 0))
    return pl.pallas_call(
        functools.partial(project_kernel, factors),
        grid=(3,),
        out_shape=[jax.ShapeDtypeStruct(shape, BF16), jax.ShapeDtypeStruct((8, 128), F32)],
        in_specs=[whole]
        + [pl.BlockSpec((768, 256), lambda i: (0, i))] * count
        + [small] * len(marks),
        out_specs=[pl.BlockSpec(shape, lambda i: (0, 0, 0, 0)), small],
        compiler_params=ALL_VMEM if not marks else PARAMS,
        cost_estimate=pl.CostEstimate(
            flops=2 * 512 * 768 * 768 * count,
            bytes_accessed=4 * 786432 * count,
            transcendentals=0,
        ),
    )(lines, *weights, *marks)


def pick_kernel(both_ref, out_ref, sem):
    copy = pltpu.make_async_copy(both_ref.at[:, SLOTS:], out_ref, sem)
    copy.start()
    copy.wait()


def pick(both):
    return pl.pallas_call(
        pick_kernel,
        out_shape=jax.ShapeDtypeStruct((GROUPS, SLOTS, 32, 1024), BF16),
        in_specs=[pl.BlockSpec(memory_space=pl.ANY)],
        out_specs=pl.BlockSpec(memory_space=pl.ANY),
        scratch_shapes=[pltpu.SemaphoreType.DMA(())],
        compiler_params=PARAMS,
    )(both)


def block(ref, slot):
    return ref[:, slot].reshape(-1, 1024)


def logits_kernel(_, both_ref, *refs):
    keys, out_ref = refs[:4], refs[4]
    for slot in range(SLOTS):
        scores = lax.dot_general(
            block(both_ref, slot),
            jnp.concatenate([block(k, slot) for k in keys], axis=0),
            (((1,), (1,)), ((), ())),
            preferred_element_type=F32,
        )
        out_ref[:, slot] = scores.astype(BF16).reshape(4, 32, 512)


def logits(mark, both, *keys):
    return pl.pallas_call(
        logits_kernel,
        out_shape=jax.ShapeDtypeStruct((4, SLOTS, 32, 512), BF16),
        compiler_params=PARAMS,
        cost_estimate=pl.CostEstimate(
            flops=2 * 3 * 128 * 512 * 1024, bytes_accessed=7 * 786432, transcendentals=0
        ),
    )(mark, both, *keys)


def reduce_kernel(terms_ref, out_ref):
    total = jnp.sum(terms_ref[...].astype(F32), axis=0).astype(BF16)
    out_ref[...] = jnp.broadcast_to(total[None], out_ref.shape)


def softmax_kernel(terms_ref, out_ref):
    total = jnp.sum(terms_ref[...].astype(F32), axis=0)
    top = jnp.max(total, axis=-1, keepdims=True)
    grown = jnp.exp(total - top)
    share = (grown / jnp.sum(grown, axis=-1, keepdims=True)).astype(BF16)
    out_ref[...] = jnp.broadcast_to(share[None], out_ref.shape)


def spread(kernel, terms):
    return pl.pallas_call(
        kernel,
        out_shape=jax.ShapeDtypeStruct((4, SLOTS, 32, 512), BF16),
        compiler_params=PARAMS,
    )(terms)


def attend_kernel(shares_ref, *refs):
    values, out_ref = refs[:-1], refs[-1]
    for slot in range(SLOTS):
        share = shares_ref[:, slot].reshape(128, 512)
        value = jnp.concatenate([block(v, slot) for v in values], axis=0)
        mixed = jnp.dot(share, value, preferred_element_type=F32)
        out_ref[:, slot] = mixed.astype(BF16).reshape(4, 32, 1024)


def attend(*arrays):
    return pl.pallas_call(
        attend_kernel,
        out_shape=jax.ShapeDtypeStruct((GROUPS, SLOTS, 32, 1024), BF16),
        compiler_params=PARAMS,
        cost_estimate=pl.CostEstimate(
            flops=2 * 3 * 128 * 512 * 1024, bytes_accessed=5 * 786432, transcendentals=0
        ),
    )(*arrays)


def finish_kernel(attended_ref, lines_ref, weight_ref, out_ref, joined_ref):
    rows, cols = 16, 32
    for pair in range(HEADS // 2):
        ends = []
        for side in range(2):
            group, slot = place(2 * pair + side)
            ends.append(attended_ref[group, slot].astype(F32))
        for step in range(rows // 2):
            left, right = (end[:, 128 * step : 128 * step + 128] for end in ends)
            low = low_lanes(left.shape)
            first = jnp.where(low, left, pltpu.roll(right, HEAD, 1))
            second = jnp.where(low, pltpu.roll(left, HEAD, 1), right)
            at = 2 * step * cols
            lanes = slice(128 * pair, 128 * pair + 128)
            joined_ref[at : at + cols, lanes] = first.astype(BF16)
            joined_ref[at + cols : at + 2 * cols, lanes] = second.astype(BF16)
    for part in range(3):
        lanes = slice(256 * part, 256 * part + 256)
        product = jnp.dot(joined_ref[...], weight_ref[:, lanes], preferred_element_type=F32)
        out_ref[:, lanes] = (lines_ref[:, lanes].astype(F32) + product).astype(BF16)


def finish(attended, lines, weight):
    return pl.pallas_call(
        finish_kernel,
        out_shape=jax.ShapeDtypeStruct((512, 768), BF16),
        scratch_shapes=[pltpu.VMEM((512, 768), BF16)],
        compiler_params=PARAMS,
    )(attended, lines, weight)


def swap(array, axis):
    return lax.ppermute(array, axis, [(0, 1), (1, 0)])


def exchange(array, axes):
    return lax.all_to_all(array, axes, 0, 0, tiled=True)


def join(*arrays):
    return lax.optimization_barrier(arrays)


def on_device(stack, asking, lookup, content, final):
    chains, columns, depth = stack.shape
    lines = stack.reshape(chains * columns, depth)
    factor = 1.0 / (math.sqrt(HEAD) * math.sqrt(256))
    keys, mark = project(lines, [lookup], (1.0,))
    both, mark = project(lines, [asking, content], (factor, 1.0), mark)
    keys, mark = join(exchange(keys, "y"), mark)
    far = swap(keys, "zl")
    both = exchange(both, "y")
    values = pick(both)
    terms = logits(mark, both, keys, swap(keys, "c"), far, swap(far, "c"))
    far = swap(values, "zl")
    terms = spread(reduce_kernel, exchange(terms, "x"))
    shares = spread(softmax_kernel, exchange(terms, "zh"))
    values = (values, swap(values, "c"), far, swap(far, "c"))
    shares = exchange(shares, "x")
    attended = exchange(attend(shares, *values), "y")
    return finish(attended, lines, final).reshape(chains, columns, depth)


def solution(mesh):
    fine = Mesh(mesh.devices.reshape(4, 4, 4, 2, 2), ("x", "zh", "y", "zl", "c"))
    spec = P(("x", "zh"), ("y", "zl", "c"), None)
    return jax.shard_map(
        on_device,
        mesh=fine,
        in_specs=(spec, P(), P(), P(), P()),
        out_specs=spec,
        check_vma=False,
    )
```

```python
import functools
import math

import jax
import jax.numpy as jnp
from jax import lax
from jax.experimental import pallas as pl
from jax.experimental.pallas import tpu as pltpu
from jax.sharding import Mesh, PartitionSpec as P

HEADS = 12
HEAD = 64
GROUPS = 4
SLOTS = 3
F32 = jnp.float32
BF16 = jnp.bfloat16
PARAMS = pltpu.CompilerParams(vmem_limit_bytes=20 * 1024 * 1024)
ALL_VMEM = pltpu.CompilerParams(vmem_limit_bytes=62 * 1024 * 1024)


def place(head):
    return (head // 2, head % 2) if head < 8 else (head - 8, 2)


def low_lanes(shape):
    return lax.broadcasted_iota(jnp.int32, shape, len(shape) - 1) < HEAD


def lay_out(lines, weight, factor, third, store):
    cols = 32
    product = jnp.dot(lines, weight, preferred_element_type=F32)
    if factor != 1.0:
        product = product * factor
    pairs = product.shape[0] // (2 * cols)
    product = product.reshape(pairs, 2, cols, 256)
    for part in range(2):
        tile = product[..., 128 * part : 128 * part + 128]
        first, second = tile[:, 0], tile[:, 1]
        low = low_lanes(first.shape)
        ends = (
            jnp.where(low, first, pltpu.roll(second, HEAD, 2)),
            jnp.where(low, pltpu.roll(first, HEAD, 2), second),
        )
        for side in range(2):
            group, slot = place(4 * third + 2 * part + side)
            for step in range(pairs):
                lanes = slice(128 * step, 128 * step + 128)
                store(group, slot, lanes, ends[side][step].astype(BF16))


def project_kernel(factors, lines_ref, *refs):
    out_ref, mark_ref = refs[-2:]
    mark_ref[...] = jnp.zeros_like(mark_ref)
    for item, factor in enumerate(factors):

        def store(group, slot, lanes, part, item=item):
            out_ref[group, item * SLOTS + slot, :, lanes] = part

        for third in range(3):
            lay_out(lines_ref[...], refs[3 * item + third][...], factor, third, store)


def project(lines, weights, factors, *marks):
    count = len(weights)
    small = pl.BlockSpec((8, 128), lambda i: (0, 0))
    thirds = [pl.BlockSpec((768, 256), lambda i, t=t: (0, t)) for t in range(3)]
    return pl.pallas_call(
        functools.partial(project_kernel, factors),
        grid=(2,),
        out_shape=[
            jax.ShapeDtypeStruct((GROUPS, count * SLOTS, 32, 1024), BF16),
            jax.ShapeDtypeStruct((8, 128), F32),
        ],
        in_specs=[pl.BlockSpec((256, 768), lambda i: (i, 0))]
        + thirds * count
        + [small] * len(marks),
        out_specs=[
            pl.BlockSpec((GROUPS, count * SLOTS, 32, 512), lambda i: (0, 0, 0, i)),
            small,
        ],
        compiler_params=PARAMS if marks else ALL_VMEM,
        cost_estimate=pl.CostEstimate(
            flops=2 * 512 * 768 * 768 * count,
            bytes_accessed=4 * 786432 * count,
            transcendentals=0,
        ),
    )(lines, *[weight for weight in weights for _ in range(3)], *marks)


def pick_kernel(both_ref, out_ref, sem):
    copy = pltpu.make_async_copy(both_ref.at[:, SLOTS:], out_ref, sem)
    copy.start()
    copy.wait()


def pick(both):
    return pl.pallas_call(
        pick_kernel,
        out_shape=jax.ShapeDtypeStruct((GROUPS, SLOTS, 32, 1024), BF16),
        in_specs=[pl.BlockSpec(memory_space=pl.ANY)],
        out_specs=pl.BlockSpec(memory_space=pl.ANY),
        scratch_shapes=[pltpu.SemaphoreType.DMA(())],
        compiler_params=PARAMS,
    )(both)


def block(ref, slot):
    return ref[:, slot].reshape(-1, 1024)


def logits_kernel(_, both_ref, *refs):
    keys, out_ref = refs[:4], refs[4]
    for slot in range(SLOTS):
        scores = lax.dot_general(
            block(both_ref, slot),
            jnp.concatenate([block(k, slot) for k in keys], axis=0),
            (((1,), (1,)), ((), ())),
            preferred_element_type=F32,
        )
        out_ref[:, slot] = scores.astype(BF16).reshape(4, 32, 512)


def logits(mark, both, *keys):
    return pl.pallas_call(
        logits_kernel,
        out_shape=jax.ShapeDtypeStruct((4, SLOTS, 32, 512), BF16),
        compiler_params=PARAMS,
        cost_estimate=pl.CostEstimate(
            flops=2 * 3 * 128 * 512 * 1024, bytes_accessed=7 * 786432, transcendentals=0
        ),
    )(mark, both, *keys)


def reduce_kernel(terms_ref, out_ref):
    total = jnp.sum(terms_ref[...].astype(F32), axis=0).astype(BF16)
    out_ref[...] = jnp.broadcast_to(total[None], out_ref.shape)


def softmax_kernel(terms_ref, out_ref):
    total = jnp.sum(terms_ref[...].astype(F32), axis=0)
    top = jnp.max(total, axis=-1, keepdims=True)
    grown = jnp.exp(total - top)
    share = (grown / jnp.sum(grown, axis=-1, keepdims=True)).astype(BF16)
    out_ref[...] = jnp.broadcast_to(share[None], out_ref.shape)


def spread(kernel, terms):
    return pl.pallas_call(
        kernel,
        out_shape=jax.ShapeDtypeStruct((4, SLOTS, 32, 512), BF16),
        compiler_params=PARAMS,
    )(terms)


def attend_kernel(shares_ref, *refs):
    values, out_ref = refs[:-1], refs[-1]
    for slot in range(SLOTS):
        share = shares_ref[:, slot].reshape(128, 512)
        value = jnp.concatenate([block(v, slot) for v in values], axis=0)
        mixed = jnp.dot(share, value, preferred_element_type=F32)
        out_ref[:, slot] = mixed.astype(BF16).reshape(4, 32, 1024)


def attend(*arrays):
    return pl.pallas_call(
        attend_kernel,
        out_shape=jax.ShapeDtypeStruct((GROUPS, SLOTS, 32, 1024), BF16),
        compiler_params=PARAMS,
        cost_estimate=pl.CostEstimate(
            flops=2 * 3 * 128 * 512 * 1024, bytes_accessed=5 * 786432, transcendentals=0
        ),
    )(*arrays)


def finish_kernel(attended_ref, lines_ref, weight_ref, out_ref, joined_ref):
    rows, cols = 16, 32
    for pair in range(HEADS // 2):
        ends = []
        for side in range(2):
            group, slot = place(2 * pair + side)
            ends.append(attended_ref[group, slot].astype(F32))
        for step in range(rows // 2):
            left, right = (end[:, 128 * step : 128 * step + 128] for end in ends)
            low = low_lanes(left.shape)
            first = jnp.where(low, left, pltpu.roll(right, HEAD, 1))
            second = jnp.where(low, pltpu.roll(left, HEAD, 1), right)
            at = 2 * step * cols
            lanes = slice(128 * pair, 128 * pair + 128)
            joined_ref[at : at + cols, lanes] = first.astype(BF16)
            joined_ref[at + cols : at + 2 * cols, lanes] = second.astype(BF16)
    for part in range(3):
        lanes = slice(256 * part, 256 * part + 256)
        product = jnp.dot(joined_ref[...], weight_ref[:, lanes], preferred_element_type=F32)
        out_ref[:, lanes] = (lines_ref[:, lanes].astype(F32) + product).astype(BF16)


def finish(attended, lines, weight):
    return pl.pallas_call(
        finish_kernel,
        out_shape=jax.ShapeDtypeStruct((512, 768), BF16),
        scratch_shapes=[pltpu.VMEM((512, 768), BF16)],
        compiler_params=PARAMS,
    )(attended, lines, weight)


def swap(array, axis):
    return lax.ppermute(array, axis, [(0, 1), (1, 0)])


def exchange(array, axes):
    return lax.all_to_all(array, axes, 0, 0, tiled=True)


def join(*arrays):
    return lax.optimization_barrier(arrays)


def on_device(stack, asking, lookup, content, final):
    chains, columns, depth = stack.shape
    lines = stack.reshape(chains * columns, depth)
    factor = 1.0 / (math.sqrt(HEAD) * math.sqrt(256))
    keys, mark = project(lines, [lookup], (1.0,))
    both, mark = project(lines, [asking, content], (factor, 1.0), mark)
    keys, mark = join(exchange(keys, "y"), mark)
    far = swap(keys, "zl")
    both = exchange(both, "y")
    values = pick(both)
    terms = logits(mark, both, keys, swap(keys, "c"), far, swap(far, "c"))
    far = swap(values, "zl")
    terms = spread(reduce_kernel, exchange(terms, "x"))
    shares = spread(softmax_kernel, exchange(terms, "zh"))
    values = (values, swap(values, "c"), far, swap(far, "c"))
    shares = exchange(shares, "x")
    attended = exchange(attend(shares, *values), "y")
    return finish(attended, lines, final).reshape(chains, columns, depth)


def solution(mesh):
    fine = Mesh(mesh.devices.reshape(4, 4, 4, 2, 2), ("x", "zh", "y", "zl", "c"))
    spec = P(("x", "zh"), ("y", "zl", "c"), None)
    return jax.shard_map(
        on_device,
        mesh=fine,
        in_specs=(spec, P(), P(), P(), P()),
        out_specs=spec,
        check_vma=False,
    )
```

```python
import functools
import math

import jax
import jax.numpy as jnp
from jax import lax
from jax.experimental import pallas as pl
from jax.experimental.pallas import tpu as pltpu
from jax.sharding import Mesh, PartitionSpec as P

HEADS = 12
HEAD = 64
GROUPS = 4
SLOTS = 3
F32 = jnp.float32
BF16 = jnp.bfloat16
PARAMS = pltpu.CompilerParams(vmem_limit_bytes=20 * 1024 * 1024)
ALL_VMEM = pltpu.CompilerParams(vmem_limit_bytes=62 * 1024 * 1024)


def place(head):
    return (head // 2, head % 2) if head < 8 else (head - 8, 2)


def low_lanes(shape):
    return lax.broadcasted_iota(jnp.int32, shape, len(shape) - 1) < HEAD


def lay_out(lines, weight, factor, third, store):
    cols = 32
    product = jnp.dot(lines, weight, preferred_element_type=F32)
    if factor != 1.0:
        product = product * factor
    pairs = product.shape[0] // (2 * cols)
    product = product.reshape(pairs, 2, cols, 256)
    for part in range(2):
        tile = product[..., 128 * part : 128 * part + 128]
        first, second = tile[:, 0], tile[:, 1]
        low = low_lanes(first.shape)
        ends = (
            jnp.where(low, first, pltpu.roll(second, HEAD, 2)),
            jnp.where(low, pltpu.roll(first, HEAD, 2), second),
        )
        for side in range(2):
            group, slot = place(4 * third + 2 * part + side)
            for step in range(pairs):
                lanes = slice(128 * step, 128 * step + 128)
                store(group, slot, lanes, ends[side][step].astype(BF16))


def project_kernel(factors, lines_ref, *refs):
    out_ref, mark_ref = refs[-2:]
    mark_ref[...] = jnp.zeros_like(mark_ref)
    for item, factor in enumerate(factors):

        def store(group, slot, lanes, part, item=item):
            out_ref[group, item * SLOTS + slot, :, lanes] = part

        for third in range(3):
            lay_out(lines_ref[...], refs[3 * item + third][...], factor, third, store)


def project(lines, weights, factors, *marks):
    count = len(weights)
    small = pl.BlockSpec((8, 128), lambda i: (0, 0))
    thirds = [pl.BlockSpec((768, 256), lambda i, t=t: (0, t)) for t in range(3)]
    return pl.pallas_call(
        functools.partial(project_kernel, factors),
        grid=(2,),
        out_shape=[
            jax.ShapeDtypeStruct((GROUPS, count * SLOTS, 32, 1024), BF16),
            jax.ShapeDtypeStruct((8, 128), F32),
        ],
        in_specs=[pl.BlockSpec((256, 768), lambda i: (i, 0))]
        + thirds * count
        + [small] * len(marks),
        out_specs=[
            pl.BlockSpec((GROUPS, count * SLOTS, 32, 512), lambda i: (0, 0, 0, i)),
            small,
        ],
        compiler_params=PARAMS if marks else ALL_VMEM,
        cost_estimate=pl.CostEstimate(
            flops=2 * 512 * 768 * 768 * count,
            bytes_accessed=4 * 786432 * count,
            transcendentals=0,
        ),
    )(lines, *[weight for weight in weights for _ in range(3)], *marks)


def pick_kernel(both_ref, out_ref, sem):
    copy = pltpu.make_async_copy(both_ref.at[:, SLOTS:], out_ref, sem)
    copy.start()
    copy.wait()


def pick(both):
    return pl.pallas_call(
        pick_kernel,
        out_shape=jax.ShapeDtypeStruct((GROUPS, SLOTS, 32, 1024), BF16),
        in_specs=[pl.BlockSpec(memory_space=pl.ANY)],
        out_specs=pl.BlockSpec(memory_space=pl.ANY),
        scratch_shapes=[pltpu.SemaphoreType.DMA(())],
        compiler_params=PARAMS,
    )(both)


def block(ref, slot):
    return ref[:, slot].reshape(-1, 1024)


def logits_kernel(_, both_ref, *refs):
    keys, out_ref = refs[:4], refs[4]
    for slot in range(SLOTS):
        scores = lax.dot_general(
            block(both_ref, slot),
            jnp.concatenate([block(k, slot) for k in keys], axis=0),
            (((1,), (1,)), ((), ())),
            preferred_element_type=F32,
        )
        scores = scores - jnp.mean(scores, axis=-1, keepdims=True)
        out_ref[:, slot] = scores.astype(BF16).reshape(4, 32, 512)


def logits(mark, both, *keys):
    return pl.pallas_call(
        logits_kernel,
        out_shape=jax.ShapeDtypeStruct((4, SLOTS, 32, 512), BF16),
        compiler_params=PARAMS,
        cost_estimate=pl.CostEstimate(
            flops=2 * 3 * 128 * 512 * 1024, bytes_accessed=7 * 786432, transcendentals=0
        ),
    )(mark, both, *keys)


def reduce_kernel(terms_ref, out_ref):
    total = jnp.sum(terms_ref[...].astype(F32), axis=0).astype(BF16)
    out_ref[...] = jnp.broadcast_to(total[None], out_ref.shape)


def softmax_kernel(terms_ref, out_ref):
    total = jnp.sum(terms_ref[...].astype(F32), axis=0)
    top = jnp.max(total, axis=-1, keepdims=True)
    grown = jnp.exp(total - top)
    share = (grown / jnp.sum(grown, axis=-1, keepdims=True)).astype(BF16)
    out_ref[...] = jnp.broadcast_to(share[None], out_ref.shape)


def spread(kernel, terms):
    return pl.pallas_call(
        kernel,
        out_shape=jax.ShapeDtypeStruct((4, SLOTS, 32, 512), BF16),
        compiler_params=PARAMS,
    )(terms)


def attend_kernel(shares_ref, *refs):
    values, out_ref = refs[:-1], refs[-1]
    for slot in range(SLOTS):
        share = shares_ref[:, slot].reshape(128, 512)
        value = jnp.concatenate([block(v, slot) for v in values], axis=0)
        mixed = jnp.dot(share, value, preferred_element_type=F32)
        out_ref[:, slot] = mixed.astype(BF16).reshape(4, 32, 1024)


def attend(*arrays):
    return pl.pallas_call(
        attend_kernel,
        out_shape=jax.ShapeDtypeStruct((GROUPS, SLOTS, 32, 1024), BF16),
        compiler_params=PARAMS,
        cost_estimate=pl.CostEstimate(
            flops=2 * 3 * 128 * 512 * 1024, bytes_accessed=5 * 786432, transcendentals=0
        ),
    )(*arrays)


def finish_kernel(attended_ref, lines_ref, weight_ref, out_ref, joined_ref):
    rows, cols = 16, 32
    for pair in range(HEADS // 2):
        ends = []
        for side in range(2):
            group, slot = place(2 * pair + side)
            ends.append(attended_ref[group, slot].astype(F32))
        for step in range(rows // 2):
            left, right = (end[:, 128 * step : 128 * step + 128] for end in ends)
            low = low_lanes(left.shape)
            first = jnp.where(low, left, pltpu.roll(right, HEAD, 1))
            second = jnp.where(low, pltpu.roll(left, HEAD, 1), right)
            at = 2 * step * cols
            lanes = slice(128 * pair, 128 * pair + 128)
            joined_ref[at : at + cols, lanes] = first.astype(BF16)
            joined_ref[at + cols : at + 2 * cols, lanes] = second.astype(BF16)
    for part in range(3):
        lanes = slice(256 * part, 256 * part + 256)
        product = jnp.dot(joined_ref[...], weight_ref[:, lanes], preferred_element_type=F32)
        out_ref[:, lanes] = (lines_ref[:, lanes].astype(F32) + product).astype(BF16)


def finish(attended, lines, weight):
    return pl.pallas_call(
        finish_kernel,
        out_shape=jax.ShapeDtypeStruct((512, 768), BF16),
        scratch_shapes=[pltpu.VMEM((512, 768), BF16)],
        compiler_params=PARAMS,
    )(attended, lines, weight)


def swap(array, axis):
    return lax.ppermute(array, axis, [(0, 1), (1, 0)])


def exchange(array, axes):
    return lax.all_to_all(array, axes, 0, 0, tiled=True)


def join(*arrays):
    return lax.optimization_barrier(arrays)


def on_device(stack, asking, lookup, content, final):
    chains, columns, depth = stack.shape
    lines = stack.reshape(chains * columns, depth)
    factor = 1.0 / (math.sqrt(HEAD) * math.sqrt(256))
    keys, mark = project(lines, [lookup], (1.0,))
    both, mark = project(lines, [asking, content], (factor, 1.0), mark)
    keys, mark = join(exchange(keys, "y"), mark)
    far = swap(keys, "zl")
    both = exchange(both, "y")
    values = pick(both)
    terms = logits(mark, both, keys, swap(keys, "c"), far, swap(far, "c"))
    far = swap(values, "zl")
    terms = spread(reduce_kernel, exchange(terms, "x"))
    shares = spread(softmax_kernel, exchange(terms, "zh"))
    values = (values, swap(values, "c"), far, swap(far, "c"))
    shares = exchange(shares, "x")
    attended = exchange(attend(shares, *values), "y")
    return finish(attended, lines, final).reshape(chains, columns, depth)


def solution(mesh):
    fine = Mesh(mesh.devices.reshape(4, 4, 4, 2, 2), ("x", "zh", "y", "zl", "c"))
    spec = P(("x", "zh"), ("y", "zl", "c"), None)
    return jax.shard_map(
        on_device,
        mesh=fine,
        in_specs=(spec, P(), P(), P(), P()),
        out_specs=spec,
        check_vma=False,
    )
```

```python
import functools
import math

import jax
import jax.numpy as jnp
from jax import lax
from jax.experimental import pallas as pl
from jax.experimental.pallas import tpu as pltpu
from jax.sharding import Mesh, PartitionSpec as P

HEADS = 12
HEAD = 64
GROUPS = 4
SLOTS = 3
F32 = jnp.float32
BF16 = jnp.bfloat16
PARAMS = pltpu.CompilerParams(vmem_limit_bytes=20 * 1024 * 1024)
ALL_VMEM = pltpu.CompilerParams(vmem_limit_bytes=62 * 1024 * 1024)


def place(head):
    return (head // 2, head % 2) if head < 8 else (head - 8, 2)


def low_lanes(shape):
    return lax.broadcasted_iota(jnp.int32, shape, len(shape) - 1) < HEAD


def lay_out(lines, weight, factor, third, store):
    cols = 32
    product = jnp.dot(lines, weight, preferred_element_type=F32)
    if factor != 1.0:
        product = product * factor
    pairs = product.shape[0] // (2 * cols)
    product = product.reshape(pairs, 2, cols, 256)
    for part in range(2):
        tile = product[..., 128 * part : 128 * part + 128]
        first, second = tile[:, 0], tile[:, 1]
        low = low_lanes(first.shape)
        ends = (
            jnp.where(low, first, pltpu.roll(second, HEAD, 2)),
            jnp.where(low, pltpu.roll(first, HEAD, 2), second),
        )
        for side in range(2):
            group, slot = place(4 * third + 2 * part + side)
            for step in range(pairs):
                lanes = slice(128 * step, 128 * step + 128)
                store(group, slot, lanes, ends[side][step].astype(BF16))


def project_kernel(factors, lines_ref, *refs):
    out_ref, mark_ref = refs[-2:]
    mark_ref[...] = jnp.zeros_like(mark_ref)
    for item, factor in enumerate(factors):

        def store(group, slot, lanes, part, item=item):
            out_ref[group, item * SLOTS + slot, :, lanes] = part

        for third in range(3):
            lay_out(lines_ref[...], refs[3 * item + third][...], factor, third, store)


def project(lines, weights, factors, *marks):
    count = len(weights)
    small = pl.BlockSpec((8, 128), lambda i: (0, 0))
    thirds = [pl.BlockSpec((768, 256), lambda i, t=t: (0, t)) for t in range(3)]
    return pl.pallas_call(
        functools.partial(project_kernel, factors),
        grid=(2,),
        out_shape=[
            jax.ShapeDtypeStruct((GROUPS, count * SLOTS, 32, 1024), BF16),
            jax.ShapeDtypeStruct((8, 128), F32),
        ],
        in_specs=[pl.BlockSpec((256, 768), lambda i: (i, 0))]
        + thirds * count
        + [small] * len(marks),
        out_specs=[
            pl.BlockSpec((GROUPS, count * SLOTS, 32, 512), lambda i: (0, 0, 0, i)),
            small,
        ],
        compiler_params=PARAMS if marks else ALL_VMEM,
        cost_estimate=pl.CostEstimate(
            flops=2 * 512 * 768 * 768 * count,
            bytes_accessed=4 * 786432 * count,
            transcendentals=0,
        ),
    )(lines, *[weight for weight in weights for _ in range(3)], *marks)


def pick_kernel(both_ref, out_ref, sem):
    copy = pltpu.make_async_copy(both_ref.at[:, SLOTS:], out_ref, sem)
    copy.start()
    copy.wait()


def pick(both):
    return pl.pallas_call(
        pick_kernel,
        out_shape=jax.ShapeDtypeStruct((GROUPS, SLOTS, 32, 1024), BF16),
        in_specs=[pl.BlockSpec(memory_space=pl.ANY)],
        out_specs=pl.BlockSpec(memory_space=pl.ANY),
        scratch_shapes=[pltpu.SemaphoreType.DMA(())],
        compiler_params=PARAMS,
    )(both)


def block(ref, slot):
    return ref[:, slot].reshape(-1, 1024)


def logits_kernel(_, __, both_ref, *refs):
    keys, out_ref = refs[:4], refs[4]
    for slot in range(SLOTS):
        scores = lax.dot_general(
            block(both_ref, slot),
            jnp.concatenate([block(k, slot) for k in keys], axis=0),
            (((1,), (1,)), ((), ())),
            preferred_element_type=F32,
        )
        out_ref[:, slot] = scores.reshape(4, 32, 512)


def logits(mark, values, both, *keys):
    return pl.pallas_call(
        logits_kernel,
        out_shape=jax.ShapeDtypeStruct((4, SLOTS, 32, 512), F32),
        in_specs=[pl.BlockSpec(memory_space=pl.ANY)] * 2
        + [pl.BlockSpec(memory_space=pltpu.VMEM)] * 5,
        compiler_params=PARAMS,
        cost_estimate=pl.CostEstimate(
            flops=2 * 3 * 128 * 512 * 1024, bytes_accessed=7 * 786432, transcendentals=0
        ),
    )(mark, values, both, *keys)


def reduce_kernel(terms_ref, out_ref):
    total = jnp.sum(terms_ref[...], axis=0)
    out_ref[...] = jnp.broadcast_to(total[None], out_ref.shape)


def softmax_kernel(terms_ref, out_ref):
    total = jnp.sum(terms_ref[...], axis=0)
    top = jnp.max(total, axis=-1, keepdims=True)
    grown = jnp.exp(total - top)
    share = (grown / jnp.sum(grown, axis=-1, keepdims=True)).astype(BF16)
    out_ref[...] = jnp.broadcast_to(share[None], out_ref.shape)


def spread(kernel, terms, dtype):
    return pl.pallas_call(
        kernel,
        out_shape=jax.ShapeDtypeStruct((4, SLOTS, 32, 512), dtype),
        compiler_params=PARAMS,
    )(terms)


def attend_kernel(shares_ref, *refs):
    values, out_ref = refs[:-1], refs[-1]
    for slot in range(SLOTS):
        share = shares_ref[:, slot].reshape(128, 512)
        value = jnp.concatenate([block(v, slot) for v in values], axis=0)
        mixed = jnp.dot(share, value, preferred_element_type=F32)
        out_ref[:, slot] = mixed.astype(BF16).reshape(4, 32, 1024)


def attend(*arrays):
    return pl.pallas_call(
        attend_kernel,
        out_shape=jax.ShapeDtypeStruct((GROUPS, SLOTS, 32, 1024), BF16),
        compiler_params=PARAMS,
        cost_estimate=pl.CostEstimate(
            flops=2 * 3 * 128 * 512 * 1024, bytes_accessed=5 * 786432, transcendentals=0
        ),
    )(*arrays)


def finish_kernel(attended_ref, lines_ref, weight_ref, out_ref, joined_ref):
    rows, cols = 16, 32
    for pair in range(HEADS // 2):
        ends = []
        for side in range(2):
            group, slot = place(2 * pair + side)
            ends.append(attended_ref[group, slot].astype(F32))
        for step in range(rows // 2):
            left, right = (end[:, 128 * step : 128 * step + 128] for end in ends)
            low = low_lanes(left.shape)
            first = jnp.where(low, left, pltpu.roll(right, HEAD, 1))
            second = jnp.where(low, pltpu.roll(left, HEAD, 1), right)
            at = 2 * step * cols
            lanes = slice(128 * pair, 128 * pair + 128)
            joined_ref[at : at + cols, lanes] = first.astype(BF16)
            joined_ref[at + cols : at + 2 * cols, lanes] = second.astype(BF16)
    for part in range(3):
        lanes = slice(256 * part, 256 * part + 256)
        product = jnp.dot(joined_ref[...], weight_ref[:, lanes], preferred_element_type=F32)
        out_ref[:, lanes] = (lines_ref[:, lanes].astype(F32) + product).astype(BF16)


def finish(attended, lines, weight):
    return pl.pallas_call(
        finish_kernel,
        out_shape=jax.ShapeDtypeStruct((512, 768), BF16),
        scratch_shapes=[pltpu.VMEM((512, 768), BF16)],
        compiler_params=PARAMS,
    )(attended, lines, weight)


def swap(array, axis):
    return lax.ppermute(array, axis, [(0, 1), (1, 0)])


def exchange(array, axes):
    return lax.all_to_all(array, axes, 0, 0, tiled=True)


def join(*arrays):
    return lax.optimization_barrier(arrays)


def on_device(stack, asking, lookup, content, final):
    chains, columns, depth = stack.shape
    lines = stack.reshape(chains * columns, depth)
    factor = 1.0 / (math.sqrt(HEAD) * math.sqrt(256))
    keys, mark = project(lines, [lookup], (1.0,))
    both, mark = project(lines, [asking, content], (factor, 1.0), mark)
    keys, mark = join(exchange(keys, "y"), mark)
    far = swap(keys, "zl")
    both = exchange(both, "y")
    values = pick(both)
    terms = logits(mark, values, both, keys, swap(keys, "c"), far, swap(far, "c"))
    terms, far = join(exchange(terms, "x"), swap(values, "zl"))
    terms = spread(reduce_kernel, terms, F32)
    shares = spread(softmax_kernel, exchange(terms, "zh"), BF16)
    values = (values, swap(values, "c"), far, swap(far, "c"))
    shares = exchange(shares, "x")
    attended = exchange(attend(shares, *values), "y")
    return finish(attended, lines, final).reshape(chains, columns, depth)


def solution(mesh):
    fine = Mesh(mesh.devices.reshape(4, 4, 4, 2, 2), ("x", "zh", "y", "zl", "c"))
    spec = P(("x", "zh"), ("y", "zl", "c"), None)
    return jax.shard_map(
        on_device,
        mesh=fine,
        in_specs=(spec, P(), P(), P(), P()),
        out_specs=spec,
        check_vma=False,
    )
```

```python
import functools
import math

import jax
import jax.numpy as jnp
from jax import lax
from jax.experimental import pallas as pl
from jax.experimental.pallas import tpu as pltpu
from jax.sharding import Mesh, PartitionSpec as P

HEADS = 12
HEAD = 64
GROUPS = 4
SLOTS = 3
F32 = jnp.float32
BF16 = jnp.bfloat16
PARAMS = pltpu.CompilerParams(vmem_limit_bytes=20 * 1024 * 1024)
ALL_VMEM = pltpu.CompilerParams(vmem_limit_bytes=62 * 1024 * 1024)


def place(head):
    return (head // 2, head % 2) if head < 8 else (head - 8, 2)


def low_lanes(shape):
    return lax.broadcasted_iota(jnp.int32, shape, len(shape) - 1) < HEAD


def lay_out(lines, weight, factor, third, store):
    cols = 32
    product = jnp.dot(lines, weight, preferred_element_type=F32)
    if factor != 1.0:
        product = product * factor
    pairs = product.shape[0] // (2 * cols)
    product = product.reshape(pairs, 2, cols, 256)
    for part in range(2):
        tile = product[..., 128 * part : 128 * part + 128]
        first, second = tile[:, 0], tile[:, 1]
        low = low_lanes(first.shape)
        ends = (
            jnp.where(low, first, pltpu.roll(second, HEAD, 2)),
            jnp.where(low, pltpu.roll(first, HEAD, 2), second),
        )
        for side in range(2):
            group, slot = place(4 * third + 2 * part + side)
            for step in range(pairs):
                lanes = slice(128 * step, 128 * step + 128)
                store(group, slot, lanes, ends[side][step].astype(BF16))


def project_kernel(factors, lines_ref, *refs):
    out_ref, mark_ref = refs[-2:]
    mark_ref[...] = jnp.zeros_like(mark_ref)
    for item, factor in enumerate(factors):

        def store(group, slot, lanes, part, item=item):
            out_ref[group, item * SLOTS + slot, :, lanes] = part

        for third in range(3):
            lay_out(lines_ref[...], refs[3 * item + third][...], factor, third, store)


def project(lines, weights, factors, *marks):
    count = len(weights)
    small = pl.BlockSpec((8, 128), lambda i: (0, 0))
    thirds = [pl.BlockSpec((768, 256), lambda i, t=t: (0, t)) for t in range(3)]
    return pl.pallas_call(
        functools.partial(project_kernel, factors),
        grid=(2,),
        out_shape=[
            jax.ShapeDtypeStruct((GROUPS, count * SLOTS, 32, 1024), BF16),
            jax.ShapeDtypeStruct((8, 128), F32),
        ],
        in_specs=[pl.BlockSpec((256, 768), lambda i: (i, 0))]
        + thirds * count
        + [small] * len(marks),
        out_specs=[
            pl.BlockSpec((GROUPS, count * SLOTS, 32, 512), lambda i: (0, 0, 0, i)),
            small,
        ],
        compiler_params=PARAMS if marks else ALL_VMEM,
        cost_estimate=pl.CostEstimate(
            flops=2 * 512 * 768 * 768 * count,
            bytes_accessed=4 * 786432 * count,
            transcendentals=0,
        ),
    )(lines, *[weight for weight in weights for _ in range(3)], *marks)


def pick_kernel(both_ref, out_ref, sem):
    copy = pltpu.make_async_copy(both_ref.at[:, SLOTS:], out_ref, sem)
    copy.start()
    copy.wait()


def pick(both):
    return pl.pallas_call(
        pick_kernel,
        out_shape=jax.ShapeDtypeStruct((GROUPS, SLOTS, 32, 1024), BF16),
        in_specs=[pl.BlockSpec(memory_space=pl.ANY)],
        out_specs=pl.BlockSpec(memory_space=pl.ANY),
        scratch_shapes=[pltpu.SemaphoreType.DMA(())],
        compiler_params=PARAMS,
    )(both)


def block(ref, slot):
    return ref[:, slot].reshape(-1, 1024)


def logits_kernel(_, both_ref, *refs):
    keys, out_ref = refs[:4], refs[4]
    for slot in range(SLOTS):
        scores = lax.dot_general(
            block(both_ref, slot),
            jnp.concatenate([block(k, slot) for k in keys], axis=0),
            (((1,), (1,)), ((), ())),
            preferred_element_type=F32,
        )
        scores = scores - jnp.mean(scores, axis=-1, keepdims=True)
        out_ref[:, slot] = scores.reshape(4, 32, 512)


def logits(mark, both, *keys):
    return pl.pallas_call(
        logits_kernel,
        out_shape=jax.ShapeDtypeStruct((4, SLOTS, 32, 512), F32),
        compiler_params=PARAMS,
        cost_estimate=pl.CostEstimate(
            flops=2 * 3 * 128 * 512 * 1024, bytes_accessed=7 * 786432, transcendentals=0
        ),
    )(mark, both, *keys)


def reduce_kernel(terms_ref, out_ref, rest_ref):
    total = jnp.sum(terms_ref[...], axis=0)
    sent = total.astype(BF16)
    out_ref[...] = jnp.broadcast_to(sent[None], out_ref.shape)
    rest_ref[...] = total - sent.astype(F32)


def softmax_kernel(terms_ref, rest_ref, out_ref):
    total = jnp.sum(terms_ref[...].astype(F32), axis=0) + rest_ref[...]
    top = jnp.max(total, axis=-1, keepdims=True)
    grown = jnp.exp(total - top)
    share = (grown / jnp.sum(grown, axis=-1, keepdims=True)).astype(BF16)
    out_ref[...] = jnp.broadcast_to(share[None], out_ref.shape)


def reduce(terms):
    return pl.pallas_call(
        reduce_kernel,
        out_shape=[
            jax.ShapeDtypeStruct((4, SLOTS, 32, 512), BF16),
            jax.ShapeDtypeStruct((SLOTS, 32, 512), F32),
        ],
        compiler_params=PARAMS,
    )(terms)


def softmax(terms, rest):
    return pl.pallas_call(
        softmax_kernel,
        out_shape=jax.ShapeDtypeStruct((4, SLOTS, 32, 512), BF16),
        compiler_params=PARAMS,
    )(terms, rest)


def attend_kernel(shares_ref, *refs):
    values, out_ref = refs[:-1], refs[-1]
    for slot in range(SLOTS):
        share = shares_ref[:, slot].reshape(128, 512)
        value = jnp.concatenate([block(v, slot) for v in values], axis=0)
        mixed = jnp.dot(share, value, preferred_element_type=F32)
        out_ref[:, slot] = mixed.astype(BF16).reshape(4, 32, 1024)


def attend(*arrays):
    return pl.pallas_call(
        attend_kernel,
        out_shape=jax.ShapeDtypeStruct((GROUPS, SLOTS, 32, 1024), BF16),
        compiler_params=PARAMS,
        cost_estimate=pl.CostEstimate(
            flops=2 * 3 * 128 * 512 * 1024, bytes_accessed=5 * 786432, transcendentals=0
        ),
    )(*arrays)


def finish_kernel(attended_ref, lines_ref, weight_ref, out_ref, joined_ref):
    rows, cols = 16, 32
    for pair in range(HEADS // 2):
        ends = []
        for side in range(2):
            group, slot = place(2 * pair + side)
            ends.append(attended_ref[group, slot].astype(F32))
        for step in range(rows // 2):
            left, right = (end[:, 128 * step : 128 * step + 128] for end in ends)
            low = low_lanes(left.shape)
            first = jnp.where(low, left, pltpu.roll(right, HEAD, 1))
            second = jnp.where(low, pltpu.roll(left, HEAD, 1), right)
            at = 2 * step * cols
            lanes = slice(128 * pair, 128 * pair + 128)
            joined_ref[at : at + cols, lanes] = first.astype(BF16)
            joined_ref[at + cols : at + 2 * cols, lanes] = second.astype(BF16)
    for part in range(3):
        lanes = slice(256 * part, 256 * part + 256)
        product = jnp.dot(joined_ref[...], weight_ref[:, lanes], preferred_element_type=F32)
        out_ref[:, lanes] = (lines_ref[:, lanes].astype(F32) + product).astype(BF16)


def finish(attended, lines, weight):
    return pl.pallas_call(
        finish_kernel,
        out_shape=jax.ShapeDtypeStruct((512, 768), BF16),
        scratch_shapes=[pltpu.VMEM((512, 768), BF16)],
        compiler_params=PARAMS,
    )(attended, lines, weight)


def swap(array, axis):
    return lax.ppermute(array, axis, [(0, 1), (1, 0)])


def exchange(array, axes):
    return lax.all_to_all(array, axes, 0, 0, tiled=True)


def join(*arrays):
    return lax.optimization_barrier(arrays)


def on_device(stack, asking, lookup, content, final):
    chains, columns, depth = stack.shape
    lines = stack.reshape(chains * columns, depth)
    factor = 1.0 / (math.sqrt(HEAD) * math.sqrt(256))
    keys, mark = project(lines, [lookup], (1.0,))
    both, mark = project(lines, [asking, content], (factor, 1.0), mark)
    keys, mark = join(exchange(keys, "y"), mark)
    far = swap(keys, "zl")
    both = exchange(both, "y")
    values = pick(both)
    terms = logits(mark, both, keys, swap(keys, "c"), far, swap(far, "c"))
    far = swap(values, "zl")
    terms, rest = reduce(exchange(terms, "x"))
    shares = softmax(exchange(terms, "zh"), rest)
    values = (values, swap(values, "c"), far, swap(far, "c"))
    shares = exchange(shares, "x")
    attended = exchange(attend(shares, *values), "y")
    return finish(attended, lines, final).reshape(chains, columns, depth)


def solution(mesh):
    fine = Mesh(mesh.devices.reshape(4, 4, 4, 2, 2), ("x", "zh", "y", "zl", "c"))
    spec = P(("x", "zh"), ("y", "zl", "c"), None)
    return jax.shard_map(
        on_device,
        mesh=fine,
        in_specs=(spec, P(), P(), P(), P()),
        out_specs=spec,
        check_vma=False,
    )
```

```python
import functools
import math

import jax
import jax.numpy as jnp
from jax import lax
from jax.experimental import pallas as pl
from jax.experimental.pallas import tpu as pltpu
from jax.sharding import Mesh, PartitionSpec as P

HEADS = 12
HEAD = 64
GROUPS = 4
SLOTS = 3
F32 = jnp.float32
BF16 = jnp.bfloat16
PARAMS = pltpu.CompilerParams(vmem_limit_bytes=20 * 1024 * 1024)
ALL_VMEM = pltpu.CompilerParams(vmem_limit_bytes=62 * 1024 * 1024)


def place(head):
    return (head // 2, head % 2) if head < 8 else (head - 8, 2)


def low_lanes(shape):
    return lax.broadcasted_iota(jnp.int32, shape, len(shape) - 1) < HEAD


def lay_out(lines, weight, factor, third, store):
    cols = 32
    product = jnp.dot(lines, weight, preferred_element_type=F32)
    if factor != 1.0:
        product = product * factor
    pairs = product.shape[0] // (2 * cols)
    product = product.reshape(pairs, 2, cols, 256)
    for part in range(2):
        tile = product[..., 128 * part : 128 * part + 128]
        first, second = tile[:, 0], tile[:, 1]
        low = low_lanes(first.shape)
        ends = (
            jnp.where(low, first, pltpu.roll(second, HEAD, 2)),
            jnp.where(low, pltpu.roll(first, HEAD, 2), second),
        )
        for side in range(2):
            group, slot = place(4 * third + 2 * part + side)
            for step in range(pairs):
                lanes = slice(128 * step, 128 * step + 128)
                store(group, slot, lanes, ends[side][step].astype(BF16))


def project_kernel(factors, lines_ref, *refs):
    out_ref, mark_ref = refs[-2:]
    mark_ref[...] = jnp.zeros_like(mark_ref)
    for item, factor in enumerate(factors):

        def store(group, slot, lanes, part, item=item):
            out_ref[group, item * SLOTS + slot, :, lanes] = part

        for third in range(3):
            lay_out(lines_ref[...], refs[3 * item + third][...], factor, third, store)


def project(lines, weights, factors, *marks):
    count = len(weights)
    small = pl.BlockSpec((8, 128), lambda i: (0, 0))
    thirds = [pl.BlockSpec((768, 256), lambda i, t=t: (0, t)) for t in range(3)]
    return pl.pallas_call(
        functools.partial(project_kernel, factors),
        grid=(2,),
        out_shape=[
            jax.ShapeDtypeStruct((GROUPS, count * SLOTS, 32, 1024), BF16),
            jax.ShapeDtypeStruct((8, 128), F32),
        ],
        in_specs=[pl.BlockSpec((256, 768), lambda i: (i, 0))]
        + thirds * count
        + [small] * len(marks),
        out_specs=[
            pl.BlockSpec((GROUPS, count * SLOTS, 32, 512), lambda i: (0, 0, 0, i)),
            small,
        ],
        compiler_params=PARAMS if marks else ALL_VMEM,
        cost_estimate=pl.CostEstimate(
            flops=2 * 512 * 768 * 768 * count,
            bytes_accessed=4 * 786432 * count,
            transcendentals=0,
        ),
    )(lines, *[weight for weight in weights for _ in range(3)], *marks)


def pick_kernel(both_ref, out_ref, sem):
    copy = pltpu.make_async_copy(both_ref.at[:, SLOTS:], out_ref, sem)
    copy.start()
    copy.wait()


def pick(both):
    return pl.pallas_call(
        pick_kernel,
        out_shape=jax.ShapeDtypeStruct((GROUPS, SLOTS, 32, 1024), BF16),
        in_specs=[pl.BlockSpec(memory_space=pl.ANY)],
        out_specs=pl.BlockSpec(memory_space=pl.ANY),
        scratch_shapes=[pltpu.SemaphoreType.DMA(())],
        compiler_params=PARAMS,
    )(both)


def block(ref, slot):
    return ref[:, slot].reshape(-1, 1024)


def logits_kernel(_, both_ref, *refs):
    keys, out_ref = refs[:4], refs[4]
    for slot in range(SLOTS):
        scores = lax.dot_general(
            block(both_ref, slot),
            jnp.concatenate([block(k, slot) for k in keys], axis=0),
            (((1,), (1,)), ((), ())),
            preferred_element_type=F32,
        )
        scores = scores - jnp.mean(scores, axis=-1, keepdims=True)
        out_ref[:, slot] = scores.astype(BF16).reshape(4, 32, 512)


def logits(mark, both, *keys):
    return pl.pallas_call(
        logits_kernel,
        out_shape=jax.ShapeDtypeStruct((4, SLOTS, 32, 512), BF16),
        compiler_params=PARAMS,
        cost_estimate=pl.CostEstimate(
            flops=2 * 3 * 128 * 512 * 1024, bytes_accessed=7 * 786432, transcendentals=0
        ),
    )(mark, both, *keys)


def reduce_kernel(terms_ref, out_ref):
    total = jnp.sum(terms_ref[...].astype(F32), axis=0).astype(BF16)
    out_ref[...] = jnp.broadcast_to(total[None], out_ref.shape)


def softmax_kernel(terms_ref, out_ref):
    total = jnp.sum(terms_ref[...].astype(F32), axis=0)
    top = jnp.max(total, axis=-1, keepdims=True)
    grown = jnp.exp(total - top)
    share = (grown / jnp.sum(grown, axis=-1, keepdims=True)).astype(BF16)
    out_ref[...] = jnp.broadcast_to(share[None], out_ref.shape)


def spread(kernel, terms):
    return pl.pallas_call(
        kernel,
        out_shape=jax.ShapeDtypeStruct((4, SLOTS, 32, 512), BF16),
        compiler_params=PARAMS,
    )(terms)


def attend_kernel(shares_ref, *refs):
    values, out_ref = refs[:-1], refs[-1]
    for slot in range(SLOTS):
        share = shares_ref[:, slot].reshape(128, 512)
        value = jnp.concatenate([block(v, slot) for v in values], axis=0)
        mixed = jnp.dot(share, value, preferred_element_type=F32)
        out_ref[:, slot] = mixed.astype(BF16).reshape(4, 32, 1024)


def attend(*arrays):
    return pl.pallas_call(
        attend_kernel,
        out_shape=jax.ShapeDtypeStruct((GROUPS, SLOTS, 32, 1024), BF16),
        compiler_params=PARAMS,
        cost_estimate=pl.CostEstimate(
            flops=2 * 3 * 128 * 512 * 1024, bytes_accessed=5 * 786432, transcendentals=0
        ),
    )(*arrays)


def finish_kernel(attended_ref, lines_ref, weight_ref, out_ref, *refs):
    joined_refs, held_refs, sems = refs[:2], refs[2:4], refs[4]
    cols = 32
    sent = []
    for half in range(2):
        joined_ref, held_ref = joined_refs[half], held_refs[half]
        rows = slice(256 * half, 256 * half + 256)
        for pair in range(HEADS // 2):
            lanes = slice(128 * pair, 128 * pair + 128)
            ends = []
            for side in range(2):
                group, slot = place(2 * pair + side)
                ends.append(attended_ref[group, slot, :, 512 * half : 512 * half + 512].astype(F32))
            for step in range(4):
                left, right = (end[:, 128 * step : 128 * step + 128] for end in ends)
                low = low_lanes(left.shape)
                first = jnp.where(low, left, pltpu.roll(right, HEAD, 1))
                second = jnp.where(low, pltpu.roll(left, HEAD, 1), right)
                at = 2 * step * cols
                joined_ref[at : at + cols, lanes] = first.astype(BF16)
                joined_ref[at + cols : at + 2 * cols, lanes] = second.astype(BF16)
        for part in range(3):
            lanes = slice(256 * part, 256 * part + 256)
            product = jnp.dot(joined_ref[...], weight_ref[:, lanes], preferred_element_type=F32)
            held_ref[:, lanes] = (lines_ref[rows, lanes].astype(F32) + product).astype(BF16)
        copy = pltpu.make_async_copy(held_ref, out_ref.at[rows], sems.at[half])
        copy.start()
        sent.append(copy)
    for copy in sent:
        copy.wait()


def finish(attended, lines, weight):
    return pl.pallas_call(
        finish_kernel,
        out_shape=jax.ShapeDtypeStruct((512, 768), BF16),
        out_specs=pl.BlockSpec(memory_space=pl.ANY),
        scratch_shapes=[pltpu.VMEM((256, 768), BF16)] * 4 + [pltpu.SemaphoreType.DMA((2,))],
        compiler_params=PARAMS,
    )(attended, lines, weight)


def swap(array, axis):
    return lax.ppermute(array, axis, [(0, 1), (1, 0)])


def exchange(array, axes):
    return lax.all_to_all(array, axes, 0, 0, tiled=True)


def join(*arrays):
    return lax.optimization_barrier(arrays)


def on_device(stack, asking, lookup, content, final):
    chains, columns, depth = stack.shape
    lines = stack.reshape(chains * columns, depth)
    factor = 1.0 / (math.sqrt(HEAD) * math.sqrt(256))
    keys, mark = project(lines, [lookup], (1.0,))
    both, mark = project(lines, [asking, content], (factor, 1.0), mark)
    keys, mark = join(exchange(keys, "y"), mark)
    far = swap(keys, "zl")
    both = exchange(both, "y")
    values = pick(both)
    terms = logits(mark, both, keys, swap(keys, "c"), far, swap(far, "c"))
    far = swap(values, "zl")
    terms = spread(reduce_kernel, exchange(terms, "x"))
    shares = spread(softmax_kernel, exchange(terms, "zh"))
    values = (values, swap(values, "c"), far, swap(far, "c"))
    shares = exchange(shares, "x")
    attended = exchange(attend(shares, *values), "y")
    return finish(attended, lines, final).reshape(chains, columns, depth)


def solution(mesh):
    fine = Mesh(mesh.devices.reshape(4, 4, 4, 2, 2), ("x", "zh", "y", "zl", "c"))
    spec = P(("x", "zh"), ("y", "zl", "c"), None)
    return jax.shard_map(
        on_device,
        mesh=fine,
        in_specs=(spec, P(), P(), P(), P()),
        out_specs=spec,
        check_vma=False,
    )
```

```python
import functools
import math

import jax
import jax.numpy as jnp
from jax import lax
from jax.experimental import pallas as pl
from jax.experimental.pallas import tpu as pltpu
from jax.sharding import Mesh, PartitionSpec as P

HEADS = 12
HEAD = 64
GROUPS = 4
SLOTS = 3
F32 = jnp.float32
BF16 = jnp.bfloat16
PARAMS = pltpu.CompilerParams(vmem_limit_bytes=20 * 1024 * 1024)
ALL_VMEM = pltpu.CompilerParams(vmem_limit_bytes=62 * 1024 * 1024)


def place(head):
    return (head // 2, head % 2) if head < 8 else (head - 8, 2)


def low_lanes(shape):
    return lax.broadcasted_iota(jnp.int32, shape, len(shape) - 1) < HEAD


def lay_out(lines_ref, weight_refs, factor, third, store):
    cols = 32
    product = sum(
        jnp.dot(
            lines_ref[:, 256 * k : 256 * k + 256],
            weight_ref[:, 256 * third : 256 * third + 256],
            preferred_element_type=F32,
        )
        for k, weight_ref in enumerate(weight_refs)
    )
    if factor != 1.0:
        product = product * factor
    pairs = product.shape[0] // (2 * cols)
    product = product.reshape(pairs, 2, cols, 256)
    for part in range(2):
        tile = product[..., 128 * part : 128 * part + 128]
        first, second = tile[:, 0], tile[:, 1]
        low = low_lanes(first.shape)
        ends = (
            jnp.where(low, first, pltpu.roll(second, HEAD, 2)),
            jnp.where(low, pltpu.roll(first, HEAD, 2), second),
        )
        for side in range(2):
            group, slot = place(4 * third + 2 * part + side)
            for step in range(pairs):
                lanes = slice(128 * step, 128 * step + 128)
                store(group, slot, lanes, ends[side][step].astype(BF16))


def project_kernel(factors, lines_ref, *refs):
    out_ref, mark_ref = refs[-2:]
    mark_ref[...] = jnp.zeros_like(mark_ref)
    for item, factor in enumerate(factors):

        def store(group, slot, lanes, part, item=item):
            out_ref[group, item * SLOTS + slot, :, lanes] = part

        for third in range(3):
            lay_out(lines_ref, refs[3 * item : 3 * item + 3], factor, third, store)


def project(lines, weights, factors, *marks):
    count = len(weights)
    small = pl.BlockSpec((8, 128), lambda i: (0, 0))
    thirds = [pl.BlockSpec((256, 768), lambda i, t=t: (t, 0)) for t in range(3)]
    return pl.pallas_call(
        functools.partial(project_kernel, factors),
        grid=(2,),
        out_shape=[
            jax.ShapeDtypeStruct((GROUPS, count * SLOTS, 32, 1024), BF16),
            jax.ShapeDtypeStruct((8, 128), F32),
        ],
        in_specs=[pl.BlockSpec((256, 768), lambda i: (i, 0))]
        + thirds * count
        + [small] * len(marks),
        out_specs=[
            pl.BlockSpec((GROUPS, count * SLOTS, 32, 512), lambda i: (0, 0, 0, i)),
            small,
        ],
        compiler_params=PARAMS if marks else ALL_VMEM,
        cost_estimate=pl.CostEstimate(
            flops=2 * 512 * 768 * 768 * count,
            bytes_accessed=4 * 786432 * count,
            transcendentals=0,
        ),
    )(lines, *[weight for weight in weights for _ in range(3)], *marks)


def pick_kernel(both_ref, out_ref, sem):
    copy = pltpu.make_async_copy(both_ref.at[:, SLOTS:], out_ref, sem)
    copy.start()
    copy.wait()


def pick(both):
    return pl.pallas_call(
        pick_kernel,
        out_shape=jax.ShapeDtypeStruct((GROUPS, SLOTS, 32, 1024), BF16),
        in_specs=[pl.BlockSpec(memory_space=pl.ANY)],
        out_specs=pl.BlockSpec(memory_space=pl.ANY),
        scratch_shapes=[pltpu.SemaphoreType.DMA(())],
        compiler_params=PARAMS,
    )(both)


def block(ref, slot):
    return ref[:, slot].reshape(-1, 1024)


def logits_kernel(_, both_ref, *refs):
    keys, out_ref = refs[:4], refs[4]
    for slot in range(SLOTS):
        scores = lax.dot_general(
            block(both_ref, slot),
            jnp.concatenate([block(k, slot) for k in keys], axis=0),
            (((1,), (1,)), ((), ())),
            preferred_element_type=F32,
        )
        scores = scores - jnp.mean(scores, axis=-1, keepdims=True)
        out_ref[:, slot] = scores.astype(BF16).reshape(4, 32, 512)


def logits(mark, both, *keys):
    return pl.pallas_call(
        logits_kernel,
        out_shape=jax.ShapeDtypeStruct((4, SLOTS, 32, 512), BF16),
        compiler_params=PARAMS,
        cost_estimate=pl.CostEstimate(
            flops=2 * 3 * 128 * 512 * 1024, bytes_accessed=7 * 786432, transcendentals=0
        ),
    )(mark, both, *keys)


def reduce_kernel(terms_ref, out_ref):
    total = jnp.sum(terms_ref[...].astype(F32), axis=0).astype(BF16)
    out_ref[...] = jnp.broadcast_to(total[None], out_ref.shape)


def softmax_kernel(terms_ref, out_ref):
    total = jnp.sum(terms_ref[...].astype(F32), axis=0)
    top = jnp.max(total, axis=-1, keepdims=True)
    grown = jnp.exp(total - top)
    share = (grown / jnp.sum(grown, axis=-1, keepdims=True)).astype(BF16)
    out_ref[...] = jnp.broadcast_to(share[None], out_ref.shape)


def spread(kernel, terms):
    return pl.pallas_call(
        kernel,
        out_shape=jax.ShapeDtypeStruct((4, SLOTS, 32, 512), BF16),
        compiler_params=PARAMS,
    )(terms)


def attend_kernel(shares_ref, *refs):
    values, out_ref = refs[:-1], refs[-1]
    for slot in range(SLOTS):
        share = shares_ref[:, slot].reshape(128, 512)
        value = jnp.concatenate([block(v, slot) for v in values], axis=0)
        mixed = jnp.dot(share, value, preferred_element_type=F32)
        out_ref[:, slot] = mixed.astype(BF16).reshape(4, 32, 1024)


def attend(*arrays):
    return pl.pallas_call(
        attend_kernel,
        out_shape=jax.ShapeDtypeStruct((GROUPS, SLOTS, 32, 1024), BF16),
        compiler_params=PARAMS,
        cost_estimate=pl.CostEstimate(
            flops=2 * 3 * 128 * 512 * 1024, bytes_accessed=5 * 786432, transcendentals=0
        ),
    )(*arrays)


def finish_kernel(attended_ref, lines_ref, weight_ref, out_ref, *refs):
    joined_refs, held_refs, sems = refs[:2], refs[2:4], refs[4]
    cols = 32
    sent = []
    for half in range(2):
        joined_ref, held_ref = joined_refs[half], held_refs[half]
        rows = slice(256 * half, 256 * half + 256)
        for pair in range(HEADS // 2):
            lanes = slice(128 * pair, 128 * pair + 128)
            ends = []
            for side in range(2):
                group, slot = place(2 * pair + side)
                ends.append(attended_ref[group, slot, :, 512 * half : 512 * half + 512].astype(F32))
            for step in range(4):
                left, right = (end[:, 128 * step : 128 * step + 128] for end in ends)
                low = low_lanes(left.shape)
                first = jnp.where(low, left, pltpu.roll(right, HEAD, 1))
                second = jnp.where(low, pltpu.roll(left, HEAD, 1), right)
                at = 2 * step * cols
                joined_ref[at : at + cols, lanes] = first.astype(BF16)
                joined_ref[at + cols : at + 2 * cols, lanes] = second.astype(BF16)
        for part in range(3):
            lanes = slice(256 * part, 256 * part + 256)
            product = jnp.dot(joined_ref[...], weight_ref[:, lanes], preferred_element_type=F32)
            held_ref[:, lanes] = (lines_ref[rows, lanes].astype(F32) + product).astype(BF16)
        copy = pltpu.make_async_copy(held_ref, out_ref.at[rows], sems.at[half])
        copy.start()
        sent.append(copy)
    for copy in sent:
        copy.wait()


def finish(attended, lines, weight):
    return pl.pallas_call(
        finish_kernel,
        out_shape=jax.ShapeDtypeStruct((512, 768), BF16),
        out_specs=pl.BlockSpec(memory_space=pl.ANY),
        scratch_shapes=[pltpu.VMEM((256, 768), BF16)] * 4 + [pltpu.SemaphoreType.DMA((2,))],
        compiler_params=PARAMS,
    )(attended, lines, weight)


def swap(array, axis):
    return lax.ppermute(array, axis, [(0, 1), (1, 0)])


def exchange(array, axes):
    return lax.all_to_all(array, axes, 0, 0, tiled=True)


def join(*arrays):
    return lax.optimization_barrier(arrays)


def on_device(stack, asking, lookup, content, final):
    chains, columns, depth = stack.shape
    lines = stack.reshape(chains * columns, depth)
    factor = 1.0 / (math.sqrt(HEAD) * math.sqrt(256))
    keys, mark = project(lines, [lookup], (1.0,))
    both, mark = project(lines, [asking, content], (factor, 1.0), mark)
    keys, mark = join(exchange(keys, "y"), mark)
    far = swap(keys, "zl")
    both = exchange(both, "y")
    values = pick(both)
    terms = logits(mark, both, keys, swap(keys, "c"), far, swap(far, "c"))
    far = swap(values, "zl")
    terms = spread(reduce_kernel, exchange(terms, "x"))
    shares = spread(softmax_kernel, exchange(terms, "zh"))
    values = (values, swap(values, "c"), far, swap(far, "c"))
    shares = exchange(shares, "x")
    attended = exchange(attend(shares, *values), "y")
    return finish(attended, lines, final).reshape(chains, columns, depth)


def solution(mesh):
    fine = Mesh(mesh.devices.reshape(4, 4, 4, 2, 2), ("x", "zh", "y", "zl", "c"))
    spec = P(("x", "zh"), ("y", "zl", "c"), None)
    return jax.shard_map(
        on_device,
        mesh=fine,
        in_specs=(spec, P(), P(), P(), P()),
        out_specs=spec,
        check_vma=False,
    )
```
